32 devices in a mesh: groups: 2 (over y), ctx: 4 (over z), tp: 4 (over x, core).
Axes of the slice: x: 2, y: 2, z: 4, core: 2. Of those that a mesh axis runs over, the one named last changes fastest.
Arguments:
- streams: bfloat16 [3, 1024, 8192], P(None, ('groups', 'ctx'), 'tp'), parts along dimension 1, may hold values from -6 to 6
- short_filter: float32 [3, 3, 8192], P(None, None, 'tp'), may hold values from -3 to 3
- decay_rate: float32 [8192, 16], P('tp'), may hold values from 0 to 1
- residue: float32 [8192, 16], P('tp'), may hold values from -0.2 to 0.2
- skip_gain: float32 [8192], P('tp'), may hold values from -4 to 4
- lengths: int32 [4], P('groups'), parts along dimension 0, may hold values from 1 to 448, 512 in all
- queries: bfloat16 [1024, 8192], P(('groups', 'ctx'), 'tp'), parts along dimension 0, may hold values from -8 to 8
- keys: bfloat16 [1024, 8192], P(('groups', 'ctx'), 'tp'), parts along dimension 0, may hold values from -8 to 8
Outputs:
- hyena_out: bfloat16 [1024, 8192], P(('groups', 'ctx'), 'tp'), parts along dimension 0
- attended: bfloat16 [1024, 8192], P(('groups', 'ctx'), 'tp'), parts along dimension 0
The draws below stay inside these ranges and needn't reach their ends.
There are 2 independent parts, one for each index of `groups`. The reference program is written for one: setup_inputs(seed, part) draws one part's arguments, and reference() takes and returns one part's arrays. A program takes and returns all parts, laid end to end along the dimension named above; an argument that names none is the same for every part. Nothing has to cross between parts.
Inputs may be any that keep to these rules, and one draw needn't show every extreme that they name: The requests fill the group in order, their lengths sum to 512, and the longest has at most 448 tokens.
All inputs are finite; a program needn't handle non-finite values.
Results may differ from the reference program's by a relative error of at most 0.01.
Values may be sent and summed in bfloat16 or wider, within the bound.
A program may use at most 128 MiB of HBM per device.

```python
import math
import jax
import jax.numpy as jnp
import numpy as np
from jax import lax

D = 8192
HEADS = 64
HEAD_DIM = 128
MODES = 16
SHORT = 3
REQS = 2
TOKENS = 512
MOST = 448


def draw_decay_rate(key, part):
    shape = (D, MODES)
    first_key = jax.random.fold_in(key, 11)
    return jnp.exp(jax.random.uniform(first_key, shape, jnp.float32, math.log(0.5 / TOKENS), math.log(1.0 / 30.0))).astype(jnp.float32)


def base_field(key, salt):
    field_key = jax.random.fold_in(key, salt)
    return jnp.clip(jax.random.normal(field_key, (TOKENS, D), jnp.float32), -6.0, 6.0)


def draw_queries(key, part):
    field = base_field(key, 1)
    return field.astype(jnp.bfloat16)


def draw_keys(key, part):
    field = base_field(key, 2)
    return field.astype(jnp.bfloat16)


def shard_levels(key, dims, shards, least, top_value):
    def one(position, blocks):
        heights = jax.random.uniform(jax.random.fold_in(jax.random.fold_in(key, 6), position), (blocks,), jnp.float32, least / len(shards), top_value / len(shards))
        return jnp.repeat(jnp.exp(heights), dims[position] // blocks).reshape((-1,) + (1,) * (len(dims) - position - 1))

    loudness = one(*shards[0])
    for cut in shards[1:]:
        loudness = loudness * one(*cut)
    return loudness


def length_profile(count, total, bound, slope):
    loads = [(1 << 20) // math.isqrt(standing ** slope) + 1 for standing in range(2, count + 1)]
    spare, given = total - bound - (count - 1), [1] * (count - 1)
    while spare > 0:
        movable = [i for i in range(count - 1) if given[i] < bound]
        whole, budget = sum([loads[i] for i in movable]), spare
        for i in movable:
            more = min(bound - given[i], max(1, budget * loads[i] // whole), spare)
            given[i] = given[i] + more
            spare = spare - more
    return np.array([bound] + given)


def ragged(stream_key, count, total, limit, lean):
    if count == 2:
        one = jax.random.randint(stream_key, (), max(1, total - limit), min(limit, total - 1) + 1)
        return jnp.stack([one, total - one])
    sizes = jnp.asarray(length_profile(count, total, limit, lean), jnp.int32)
    couples = (count - 1) // 2
    giver, taker = sizes[1:1 + 2 * couples:2], sizes[2:2 + 2 * couples:2]
    margin = jnp.minimum(giver - 1, limit - taker)
    moved = jax.random.randint(jax.random.fold_in(stream_key, 1), (couples,), 0, 1 << 20) % (margin + 1)
    sizes = sizes.at[1:1 + 2 * couples:2].set(giver - moved).at[2:2 + 2 * couples:2].set(taker + moved)
    return sizes[jax.random.permutation(jax.random.fold_in(stream_key, 2), count)]


def gaussian(stream_key, shape, scale, reach, split=(), kind=jnp.bfloat16):
    result = scale * jax.random.normal(stream_key, shape, jnp.float32)
    if split:
        result = result * shard_levels(stream_key, shape, split, -0.22, 0.18)
    return jnp.clip(result, -reach, reach).astype(kind)


def setup_inputs(seed: int = 0, part: int = 0) -> dict:
    splits = jax.random.split(jax.random.key(seed), 9)
    part_splits = jax.random.split(jax.random.fold_in(splits[8], part), 9)
    return {
        "streams": gaussian(part_splits[0], (3, TOKENS, D), 1.0, 6.0, ((1, 4), (2, 4))),
        "short_filter": gaussian(splits[1], (SHORT, 3, D), 0.6, 3.0, ((2, 4),), jnp.float32),
        "decay_rate": draw_decay_rate(jax.random.fold_in(splits[8], 71), part),
        "residue": gaussian(splits[3], (D, MODES), 0.03, 0.2, ((0, 4),), jnp.float32),
        "skip_gain": gaussian(splits[4], (D,), 1.0, 4.0, ((0, 4),), jnp.float32),
        "lengths": ragged(part_splits[5], REQS, TOKENS, MOST, 2).astype(jnp.int32),
        "queries": draw_queries(jax.random.fold_in(jax.random.fold_in(splits[8], part), 71), part),
        "keys": draw_keys(jax.random.fold_in(jax.random.fold_in(splits[8], part), 71), part),
    }


def documents(lengths):
    ends = jnp.cumsum(lengths).astype(jnp.int32)
    places = jnp.arange(TOKENS, dtype=jnp.int32)
    return lax.optimization_barrier(jnp.sum((places[:, None] >= ends[None, :]).astype(jnp.int32), axis=1)).astype(jnp.int32)

def reference(streams, short_filter, decay_rate, residue, skip_gain, lengths, queries, keys):
    document = documents(lengths)
    data = streams.astype(jnp.float32)
    filtered = jnp.zeros(data.shape, jnp.float32)
    for tap in range(SHORT):
        shifted = jnp.pad(data, ((0, 0), (tap, 0), (0, 0)))[:, :TOKENS, :]
        doc_shift = jnp.pad(document, (tap, 0), constant_values=-1)[:TOKENS]
        same = (doc_shift == document).astype(jnp.float32)
        filtered = filtered + short_filter[tap][:, None, :] * shifted * same[None, :, None]
    mixed = filtered[1] * filtered[2]
    decay = jnp.exp(-decay_rate)
    linked = jnp.concatenate([jnp.zeros((1,), jnp.float32), (document[1:] == document[:-1]).astype(jnp.float32)])

    def advance(state, inputs):
        row, flag = inputs
        state = state * decay * flag + row[:, None]
        return (state, lax.optimization_barrier(jnp.sum(residue * state, axis=1)))
    _, long = lax.scan(advance, jnp.zeros((D, MODES), jnp.float32), (mixed, linked))
    long = long + skip_gain[None, :] * mixed
    hyena_out = (filtered[0] * long).astype(jnp.bfloat16)
    scale = 1.0 / math.sqrt(HEAD_DIM)
    places = jnp.arange(TOKENS, dtype=jnp.int32)
    allowed = (places[None, :] <= places[:, None]) & (document[None, :] == document[:, None])
    query_heads = queries.reshape(TOKENS, HEADS, HEAD_DIM).transpose(1, 0, 2)
    key_heads = keys.reshape(TOKENS, HEADS, HEAD_DIM).transpose(1, 0, 2)
    value_heads = hyena_out.reshape(TOKENS, HEADS, HEAD_DIM).transpose(1, 0, 2)

    def one_head(items):
        query, key, value = items
        scores = jnp.dot(query.astype(jnp.float32), key.astype(jnp.float32).T, precision=lax.Precision.HIGHEST) * scale
        top = lax.optimization_barrier(jnp.max(jnp.where(allowed, scores, -jnp.inf), axis=1))
        weight = jnp.where(allowed, jnp.exp(scores - top[:, None]), 0.0)
        total = lax.optimization_barrier(jnp.sum(weight, axis=1))
        weight_low = lax.optimization_barrier(weight.astype(jnp.bfloat16)).astype(jnp.float32)
        summed = jnp.dot(weight_low, value.astype(jnp.float32), precision=lax.Precision.HIGHEST)
        return summed / total[:, None]
    heads_out = lax.map(one_head, (query_heads, key_heads, value_heads))
    attended = heads_out.transpose(1, 0, 2).reshape(TOKENS, D).astype(jnp.bfloat16)
    return (hyena_out, attended)
```

```python
import functools
import math

import jax
import jax.numpy as jnp
from jax import lax
from jax.experimental import pallas as pl
from jax.experimental.pallas import tpu as pltpu
from jax.sharding import PartitionSpec as P

HEAD_DIM = 128
SHORT = 3


def shifted(value, axis, steps):
    count = lax.axis_size(axis)
    leading, last = (max(0, -steps), min(count, count - steps))
    return lax.ppermute(value, axis, [(source, source + steps) for source in range(leading, last)])


def prefix(shard, axis, join, neutral):
    place = lax.axis_index(axis)
    gathered = jax.tree.map(
        lambda a, kind: lax.all_gather(a.astype(kind), axis),
        shard,
        (jnp.bfloat16, jnp.bfloat16, jnp.bfloat16),
    )
    state = jax.tree.map(lambda a, e: jnp.zeros_like(a) + jnp.asarray(e, a.dtype), shard, neutral)

    def one(step, state):
        return join(
            state,
            jax.tree.map(
                lambda a, own: lax.dynamic_index_in_dim(a, step, 0, False).astype(own.dtype),
                gathered,
                shard,
            ),
        )

    return lax.fori_loop(0, place, one, state)


def doc_of(places, ends):
    return jnp.sum((places[:, None] >= ends[None, :]).astype(jnp.int32), axis=1)


def shards(streams, short_filter, decay_rate, residue, skip_gain, lengths, queries, keys):
    rows = streams.shape[1]
    width = streams.shape[2]
    modes = decay_rate.shape[1]
    index = lax.axis_index("ctx")
    first = index * rows
    ends = jnp.cumsum(lengths)
    places = first + jnp.arange(rows, dtype=jnp.int32)
    doc_here = doc_of(places, ends)
    doc_before = doc_of(jnp.reshape(first - 1, (1,)), ends)[0]
    reach_back = SHORT - 1
    rim = shifted(streams[:, rows - reach_back :, :], "ctx", 1)
    extended = jnp.concatenate([rim, streams], axis=1)
    doc_ext = doc_of(first - reach_back + jnp.arange(rows + reach_back, dtype=jnp.int32), ends)
    filtered = jnp.zeros(streams.shape, jnp.float32)
    for tap in range(SHORT):
        window = extended[:, reach_back - tap : reach_back - tap + rows, :].astype(jnp.float32)
        same = (doc_ext[reach_back - tap : reach_back - tap + rows] == doc_here).astype(jnp.float32)
        filtered = filtered + short_filter[tap][:, None, :] * window * same[None, :, None]
    mixed = filtered[1] * filtered[2]
    sub_len = math.gcd(rows, 16)
    blocks = rows // sub_len
    lags = jnp.arange(sub_len + 1, dtype=jnp.float32)
    powers = jnp.exp(-decay_rate[None] * lags[:, None, None])
    kernel = jnp.sum(residue[None] * powers[:sub_len], axis=2)
    padded = jnp.concatenate([kernel[::-1], jnp.zeros_like(kernel)], axis=0)
    tiled = jnp.tile(padded, (sub_len, 1))[: sub_len * (2 * sub_len - 1)]
    toeplitz = tiled.reshape(sub_len, 2 * sub_len - 1, width)[:, sub_len - 1 :, :]
    mixed_blocks = mixed.reshape(blocks, sub_len, width)
    doc_blocks = doc_here.reshape(blocks, sub_len)
    same_blocks = (doc_blocks[:, :, None] == doc_blocks[:, None, :]).astype(jnp.float32)
    local = jnp.sum(toeplitz[None] * same_blocks[..., None] * mixed_blocks[:, None, :, :], axis=2)
    prior = jnp.concatenate([doc_before.reshape(1), doc_blocks[:-1, -1]])
    in_last = (doc_blocks == doc_blocks[:, -1:]).astype(jnp.float32)
    ahead = powers[sub_len:0:-1]
    summaries = jnp.einsum(
        "bjc,jcm->bcm", mixed_blocks * in_last[..., None], ahead, precision=lax.Precision.HIGHEST
    )
    keeps = (doc_blocks[:, -1] == prior).astype(jnp.float32)
    step_decay = powers[sub_len]

    def advance(carry, item):
        state, factor = carry
        summary, keep = item
        gain = step_decay * keep
        return ((state * gain + summary, factor * gain), (state, factor))

    empty_state = jnp.zeros((width, modes), jnp.float32)
    (own_state, own_factor), (pre_state, pre_factor) = lax.scan(
        advance, (empty_state, jnp.ones((width, modes), jnp.float32)), (summaries, keeps)
    )
    keep_device = jnp.prod(keeps)

    def combine(earlier, later):
        state_a, keep_a, count_a = earlier
        state_b, keep_b, count_b = later
        span = jnp.exp(-decay_rate * (rows * count_b))
        return (state_a * span * keep_b + state_b, keep_a * keep_b, count_a + count_b)

    incoming, keep_sum, count_sum = prefix(
        (own_state, keep_device, jnp.ones((), jnp.float32)),
        "ctx",
        combine,
        (empty_state, jnp.ones((), jnp.float32), jnp.zeros((), jnp.float32)),
    )
    starts = pre_state + pre_factor * incoming[None]
    carry_mask = (doc_blocks == prior[:, None]).astype(jnp.float32)
    cross = (
        jnp.einsum(
            "jcm,bcm->bjc",
            powers[:sub_len],
            residue[None] * starts,
            precision=lax.Precision.HIGHEST,
        )
        * carry_mask[..., None]
    )
    long = (local + cross).reshape(rows, width) + skip_gain[None, :] * mixed
    hyena_out = (filtered[0] * long).astype(jnp.bfloat16)
    heads_here = width // HEAD_DIM
    scale = 1.0 / math.sqrt(HEAD_DIM)
    query_docs = doc_of(places, ends)
    query_heads = queries.reshape(rows, heads_here, HEAD_DIM)
    paired = jnp.stack([keys, hyena_out])
    start_carry = (
        jnp.full((heads_here, rows), -1e30, jnp.float32),
        jnp.zeros((heads_here, rows), jnp.float32),
        jnp.zeros((heads_here, rows, HEAD_DIM), jnp.float32),
    )
    piece = lax.all_gather(paired, "ctx", axis=1, tiled=True)
    count = piece.shape[1]
    key_places = jnp.arange(count, dtype=jnp.int32)
    key_docs = doc_of(key_places, ends)
    allowed = (key_places[None, :] <= places[:, None]) & (key_docs[None, :] == query_docs[:, None])

    def compute(state):
        top, total, summed = state
        key_heads = piece[0].reshape(count, heads_here, HEAD_DIM)
        value_heads = piece[1].reshape(count, heads_here, HEAD_DIM)
        scores = jnp.einsum(
            "qhd,khd->hqk", query_heads, key_heads, preferred_element_type=jnp.float32
        )
        masked = jnp.where(allowed[None], scores * scale, -1e30)
        new_top = jnp.maximum(top, jnp.max(masked, axis=2))
        weight = jnp.exp(masked - new_top[..., None])
        total = jnp.sum(weight, axis=2)
        summed = jnp.einsum(
            "hqk,khd->hqd",
            weight.astype(jnp.bfloat16),
            value_heads,
            preferred_element_type=jnp.float32,
        )
        return (new_top, total, summed)

    def unchanged(state):
        return state

    result = lax.cond(jnp.any(allowed), compute, unchanged, start_carry)
    top, total, summed = result
    attended_rows = (
        (summed / total[..., None]).transpose(1, 0, 2).reshape(rows, width).astype(jnp.bfloat16)
    )
    return (hyena_out, attended_rows)


LANES = 128
SEGS = 8
PARTS = 4
NEG = -1e30
DIMS = (((1,), (1,)), ((), ()))


def fused_kernel(
    lengths, streams, taps, rate, residue, skip, queries, keys, hyena, attended,
    ext, rim_out, rim_in, same, mixed_seg, gate_seg, starts, own, own_low, state_in, incoming,
    tokens, query_in, key_in, value_in, part_out, part_in, lse_out, lse_in, own_part, lse_rows, bias,
    rim_s, rim_r, state_s, state_r, query_s, query_r, key_s, key_r, value_s, value_r,
    part_s, part_r, lse_s, lse_r,
):
    me = lax.axis_index("ctx")
    rows, width = queries.shape
    heads = width // LANES
    modes = rate.shape[0]
    seg = rows // SEGS
    group = width // PARTS
    per = heads // PARTS
    first = me * rows

    def send(src, dst, s, r, to):
        return pltpu.make_async_remote_copy(
            src_ref=src, dst_ref=dst, send_sem=s, recv_sem=r,
            device_id={"ctx": to}, device_id_type=pl.DeviceIdType.MESH,
        )

    def cols(g):
        return pl.ds(g * group, group)

    def rim_copy(to):
        return send(rim_out, rim_in, rim_s, rim_r, to)

    def state_copy(source, to):
        return send(own_low, state_in.at[source], state_s.at[to], state_r.at[source], to)

    def query_copy(slot, g, to):
        return send(
            queries.at[:, cols(g)], query_in.at[slot, :, cols(g)],
            query_s.at[to, g], query_r.at[slot, g], to,
        )

    def key_copy(g):
        return send(keys.at[:, cols(g)], key_in.at[:, cols(g)], key_s.at[g], key_r.at[g], 1)

    def value_copy(g):
        return send(hyena.at[:, cols(g)], value_in.at[:, cols(g)], value_s.at[g], value_r.at[g], 1)

    def part_copy(slot, source, g, to):
        return send(
            part_out.at[slot, :, cols(g)], part_in.at[source - 1, :, cols(g)],
            part_s.at[slot, g], part_r.at[source - 1, g], to,
        )

    def lse_copy(slot, source, to):
        return send(lse_out.at[slot], lse_in.at[source - 1], lse_s.at[slot], lse_r.at[source - 1], to)

    barrier = pltpu.get_barrier_semaphore()
    for away in range(1, 4):
        pl.semaphore_signal(
            barrier, inc=1, device_id={"ctx": lax.rem(me + away, 4)},
            device_id_type=pl.DeviceIdType.MESH,
        )
    for j in range(3):
        rim_out[2 * j : 2 * j + 2, :] = streams[j, rows - 16 :, :].astype(jnp.float32)[14:16]
    rim_out[6:8, :] = jnp.zeros((2, width), jnp.float32)
    pl.semaphore_wait(barrier, 3)

    for i in range(3):
        @pl.when(me == i)
        def _():
            rim_copy(i + 1).start()

    @pl.when(me == 0)
    def _():
        for g in range(PARTS):
            key_copy(g).start()

    @pl.when(me == 2)
    def _():
        for g in range(PARTS):
            query_copy(0, g, 1).start()

    @pl.when(me == 3)
    def _():
        for g in range(PARTS):
            query_copy(1, g, 1).start()
            query_copy(1, g, 2).start()

    ends = []
    total = jnp.int32(0)
    for r in range(lengths.shape[0]):
        total = total + lengths[r]
        ends.append(total)

    def doc(places):
        found = jnp.zeros(places.shape, jnp.int32)
        for end in ends:
            found = found + (places >= end).astype(jnp.int32)
        return found

    def equal(a, b):
        return (doc(a) == doc(b)).astype(jnp.float32)

    segment = lax.broadcasted_iota(jnp.int32, (SEGS, LANES), 0)
    for t in range(seg):
        at = first + segment * seg + t
        same[0, t] = equal(at, at - 1)
        same[1, t] = equal(at, at - 2)
    last = first + segment * seg + (seg - 1)
    windows = [
        equal(last, last - span * seg) * (segment >= span).astype(jnp.float32) for span in (1, 2, 4)
    ]
    before = segment * 0 + (first - 1)
    carried = equal(first + segment * seg - 1, before)

    def widen(h, _):
        lanes = pl.ds(pl.multiple_of(h * LANES, LANES), LANES)
        for j in range(3):
            ext[j, h, 8:, :] = streams[j, :, lanes].astype(jnp.float32)
        return _

    lax.fori_loop(0, heads, widen, 0)

    @pl.when(me == 0)
    def _():
        rim_in[...] = jnp.zeros(rim_in.shape, jnp.float32)

    for i in range(1, 4):
        @pl.when(me == i)
        def _():
            rim_copy(i - 1).wait_recv()

    def spread(value):
        return jnp.broadcast_to(value[:, None, :], (modes, SEGS, LANES))

    def forward(h, _):
        lanes = pl.ds(pl.multiple_of(h * LANES, LANES), LANES)
        for j in range(3):
            ext[j, h, 6:8, :] = rim_in[2 * j : 2 * j + 2, lanes]
        speed = rate[:, lanes]
        decay = spread(jnp.exp(-speed))
        gains = [
            [jnp.broadcast_to(taps[i, j : j + 1, lanes], (SEGS, LANES)) for j in range(3)]
            for i in range(3)
        ]
        older = [ext[j, h, pl.ds(6, SEGS, stride=seg), :] for j in range(3)]
        newer = [ext[j, h, pl.ds(7, SEGS, stride=seg), :] for j in range(3)]
        state = jnp.zeros((modes, SEGS, LANES), jnp.float32)
        for t in range(seg):
            here = [ext[j, h, pl.ds(8 + t, SEGS, stride=seg), :] for j in range(3)]
            near, far = same[0, t], same[1, t]
            out = [
                gains[0][j] * here[j] + gains[1][j] * (newer[j] * near) + gains[2][j] * (older[j] * far)
                for j in range(3)
            ]
            mixed = out[1] * out[2]
            gate_seg[h, t] = out[0]
            mixed_seg[h, t] = mixed
            state = state * near[None] * decay + mixed[None]
            older, newer = newer, here
        for window, span in zip(windows, (1, 2, 4)):
            step = spread(jnp.exp(-speed * float(span * seg)))
            state = state + step * window[None] * pltpu.roll(state, span, 1)
        for m in range(modes):
            own[m : m + 1, lanes] = state[m, SEGS - 1 :, :]
        starts[h] = pltpu.roll(state, 1, 1) * (segment >= 1).astype(jnp.float32)[None]
        return _

    lax.fori_loop(0, heads, forward, 0)
    own_low[...] = own[...].astype(jnp.bfloat16)
    for i in range(3):
        @pl.when(me == i)
        def _():
            for to in range(i + 1, 4):
                state_copy(i, to).start()

    incoming[...] = jnp.zeros(incoming.shape, jnp.float32)
    edge = jnp.zeros((1, LANES), jnp.int32)
    for i in range(1, 4):
        @pl.when(me == i)
        def _():
            for j in range(i - 1, -1, -1):
                state_copy(j, i).wait_recv()
                linked = equal(edge + (j + 1) * rows - 1, edge + i * rows - 1)
                linked = jnp.concatenate([linked] * heads, axis=1)
                span = jnp.exp(-rate[...] * float(rows * (i - 1 - j))) * linked
                incoming[...] = incoming[...] + state_in[j].astype(jnp.float32) * span

    age = (segment * seg).astype(jnp.float32)

    def backward(h, _):
        lanes = pl.ds(pl.multiple_of(h * LANES, LANES), LANES)
        speed = spread(rate[:, lanes])
        decay = jnp.exp(-speed)
        weight = spread(residue[:, lanes])
        direct = jnp.broadcast_to(skip[:, lanes], (SEGS, LANES))
        state = starts[h] + spread(incoming[:, lanes]) * (jnp.exp(-speed * age[None]) * carried[None])
        for t in range(seg):
            mixed = mixed_seg[h, t]
            state = state * same[0, t][None] * decay + mixed[None]
            long = jnp.sum(weight * state, axis=0) + direct * mixed
            tokens[pl.ds(t, SEGS, stride=seg), :] = gate_seg[h, t] * long
        hyena[:, lanes] = tokens[...].astype(jnp.bfloat16)
        return _

    for g in range(PARTS):
        lax.fori_loop(g * per, (g + 1) * per, backward, 0)

        @pl.when(me == 0)
        def _():
            value_copy(g).start()

    scale = 1.0 / math.sqrt(HEAD_DIM)
    lane = lax.broadcasted_iota(jnp.int32, (rows, LANES), 1)
    down = lax.broadcasted_iota(jnp.int32, (rows, rows), 0)
    across = lax.broadcasted_iota(jnp.int32, (rows, rows), 1)
    lse_rows[...] = jnp.zeros(lse_rows.shape, jnp.float32)

    def set_bias(query_block, key_block, a, b):
        p = query_block * rows + down
        q = key_block * rows + across
        allowed = (q <= p) & (doc(p) == doc(q))
        bias[a * rows : (a + 1) * rows, b * rows : (b + 1) * rows] = jnp.where(allowed, 0.0, NEG)

    def attend(query, key, value, penalty):
        scores = lax.dot_general(query, key, DIMS, preferred_element_type=jnp.float32)
        scores = scores * scale + penalty
        top = jnp.max(scores, axis=1, keepdims=True)
        weight = jnp.exp(scores - top)
        total = jnp.sum(weight, axis=1, keepdims=True)
        summed = jnp.dot(weight.astype(jnp.bfloat16), value, preferred_element_type=jnp.float32)
        return summed * (1.0 / total), top + jnp.log(total)

    def note(slot, h, value):
        lse_rows[slot] = jnp.where(lane == h, value, lse_rows[slot])

    def head_lanes(h):
        return pl.ds(pl.multiple_of(h * LANES, LANES), LANES)

    def combine(sources):
        tables = [lse_rows[0]]
        for source in sources:
            lse_copy(0, source, 0).wait_recv()
            filler = jnp.zeros((LANES - heads, rows), jnp.float32)
            tables.append(jnp.concatenate([lse_in[source - 1], filler], axis=0).T)
        peak = functools.reduce(jnp.maximum, tables)
        shares = [jnp.exp(table - peak) for table in tables]
        norm = 1.0 / functools.reduce(jnp.add, shares)
        shares = [share * norm for share in shares]
        for g in range(PARTS):
            for source in sources:
                part_copy(0, source, g, 0).wait_recv()
            for h in range(g * per, (g + 1) * per):
                at = slice(h * LANES, (h + 1) * LANES)
                whole = own_part[:, at] * shares[0][:, h : h + 1]
                for share, source in zip(shares[1:], sources):
                    whole = whole + part_in[source - 1, :, at].astype(jnp.float32) * share[:, h : h + 1]
                attended[:, at] = whole.astype(jnp.bfloat16)

    @pl.when(me == 0)
    def _():
        set_bias(0, 0, 0, 0)

        def one(h, _):
            at = head_lanes(h)
            out, lse = attend(queries[:, at], keys[:, at], hyena[:, at], bias[:rows, :rows])
            attended[:, at] = out.astype(jnp.bfloat16)
            return _

        lax.fori_loop(0, heads, one, 0)
        for g in range(PARTS):
            key_copy(g).wait_send()
            value_copy(g).wait_send()

    @pl.when(me == 1)
    def _():
        for a in range(3):
            for b in range(2):
                set_bias(a + 1, b, a, b)

        def one(h, _):
            at = head_lanes(h)
            query = jnp.concatenate([query_in[0, :, at], query_in[1, :, at], queries[:, at]], axis=0)
            key = jnp.concatenate([key_in[:, at], keys[:, at]], axis=0)
            value = jnp.concatenate([value_in[:, at], hyena[:, at]], axis=0)
            penalty = jnp.concatenate([bias[rows:, :], bias[:rows, :]], axis=0)
            out, lse = attend(query, key, value, penalty)
            part_out[0, :, at] = out[:rows].astype(jnp.bfloat16)
            part_out[1, :, at] = out[rows : 2 * rows].astype(jnp.bfloat16)
            attended[:, at] = out[2 * rows :].astype(jnp.bfloat16)
            note(0, h, lse[:rows])
            note(1, h, lse[rows : 2 * rows])
            return _

        for g in range(PARTS):
            query_copy(0, g, 1).wait_recv()
            query_copy(1, g, 1).wait_recv()
            key_copy(g).wait_recv()
            value_copy(g).wait_recv()
            lax.fori_loop(g * per, (g + 1) * per, one, 0)
            part_copy(0, 1, g, 2).start()
            part_copy(1, 1, g, 3).start()
        for slot in range(2):
            lse_out[slot] = lse_rows[slot].T[:heads]
            lse_copy(slot, 1, slot + 2).start()
        for slot in range(2):
            for g in range(PARTS):
                part_copy(slot, 1, g, slot + 2).wait_send()
            lse_copy(slot, 1, slot + 2).wait_send()

    @pl.when(me == 2)
    def _():
        set_bias(3, 2, 0, 0)
        set_bias(2, 2, 1, 0)

        def one(h, _):
            at = head_lanes(h)
            query = jnp.concatenate([query_in[1, :, at], queries[:, at]], axis=0)
            out, lse = attend(query, keys[:, at], hyena[:, at], bias[: 2 * rows, :rows])
            part_out[0, :, at] = out[:rows].astype(jnp.bfloat16)
            own_part[:, at] = out[rows:]
            note(1, h, lse[:rows])
            note(0, h, lse[rows:])
            return _

        for g in range(PARTS):
            query_copy(1, g, 2).wait_recv()
            lax.fori_loop(g * per, (g + 1) * per, one, 0)
            part_copy(0, 2, g, 3).start()
        lse_out[0] = lse_rows[1].T[:heads]
        lse_copy(0, 2, 3).start()
        combine((1,))
        for g in range(PARTS):
            query_copy(0, g, 1).wait_send()
            part_copy(0, 2, g, 3).wait_send()
        lse_copy(0, 2, 3).wait_send()

    @pl.when(me == 3)
    def _():
        set_bias(3, 3, 0, 0)

        def one(h, _):
            at = head_lanes(h)
            out, lse = attend(queries[:, at], keys[:, at], hyena[:, at], bias[:rows, :rows])
            own_part[:, at] = out
            note(0, h, lse)
            return _

        lax.fori_loop(0, heads, one, 0)
        combine((2, 1))
        for g in range(PARTS):
            query_copy(1, g, 1).wait_send()
            query_copy(1, g, 2).wait_send()

    for i in range(3):
        @pl.when(me == i)
        def _():
            rim_copy(i + 1).wait_send()
            for to in range(i + 1, 4):
                state_copy(i, to).wait_send()


def fused(streams, short_filter, decay_rate, residue, skip_gain, lengths, queries, keys):
    rows, width = queries.shape
    heads = width // LANES
    modes = decay_rate.shape[1]
    seg = rows // SEGS
    f32, bf16 = jnp.float32, jnp.bfloat16
    vmem, dma = pltpu.VMEM, pltpu.SemaphoreType.DMA
    block = pl.BlockSpec(memory_space=pltpu.VMEM)
    out = jax.ShapeDtypeStruct((rows, width), bf16)
    return pl.pallas_call(
        fused_kernel,
        out_shape=(out, out),
        in_specs=[pl.BlockSpec(memory_space=pltpu.SMEM)] + [block] * 7,
        out_specs=(block, block),
        scratch_shapes=[
            vmem((3, heads, rows + 8, LANES), f32),
            vmem((8, width), f32),
            vmem((8, width), f32),
            vmem((2, seg, SEGS, LANES), f32),
            vmem((heads, seg, SEGS, LANES), f32),
            vmem((heads, seg, SEGS, LANES), f32),
            vmem((heads, modes, SEGS, LANES), f32),
            vmem((modes, width), f32),
            vmem((modes, width), bf16),
            vmem((3, modes, width), bf16),
            vmem((modes, width), f32),
            vmem((rows, LANES), f32),
            vmem((2, rows, width), bf16),
            vmem((rows, width), bf16),
            vmem((rows, width), bf16),
            vmem((2, rows, width), bf16),
            vmem((2, rows, width), bf16),
            vmem((2, heads, rows), f32),
            vmem((2, heads, rows), f32),
            vmem((rows, width), f32),
            vmem((2, rows, LANES), f32),
            vmem((3 * rows, 2 * rows), f32),
            dma, dma, dma((4,)), dma((3,)), dma((4, PARTS)), dma((2, PARTS)),
            dma((PARTS,)), dma((PARTS,)), dma((PARTS,)), dma((PARTS,)),
            dma((2, PARTS)), dma((2, PARTS)), dma((2,)), dma((2,)),
        ],
        compiler_params=pltpu.CompilerParams(
            collective_id=0, has_side_effects=True, vmem_limit_bytes=48 * 1024 * 1024
        ),
        cost_estimate=pl.CostEstimate(
            flops=12 * rows * rows * width, bytes_accessed=14 * rows * width, transcendentals=0
        ),
    )(
        lengths, streams, short_filter, decay_rate.T, residue.T, skip_gain.reshape(1, width),
        queries, keys,
    )


def chosen(streams, *rest):
    if lax.axis_size("ctx") == 4 and streams.shape[1] == 128 and streams.shape[2] % 512 == 0:
        return fused(streams, *rest)
    return shards(streams, *rest)


def solution(mesh):
    placed = (
        P(None, ("groups", "ctx"), "tp"),
        P(None, None, "tp"),
        P("tp", None),
        P("tp", None),
        P("tp"),
        P("groups"),
        P(("groups", "ctx"), "tp"),
        P(("groups", "ctx"), "tp"),
    )
    return jax.shard_map(
        chosen,
        mesh=mesh,
        in_specs=placed,
        out_specs=(P(("groups", "ctx"), "tp"), P(("groups", "ctx"), "tp")),
        check_vma=False,
    )
```

```python
import functools
import math

import jax
import jax.numpy as jnp
from jax import lax
from jax.experimental import pallas as pl
from jax.experimental.pallas import tpu as pltpu
from jax.sharding import PartitionSpec as P

HEAD_DIM = 128
SHORT = 3


def shifted(value, axis, steps):
    count = lax.axis_size(axis)
    leading, last = (max(0, -steps), min(count, count - steps))
    return lax.ppermute(value, axis, [(source, source + steps) for source in range(leading, last)])


def prefix(shard, axis, join, neutral):
    place = lax.axis_index(axis)
    gathered = jax.tree.map(
        lambda a, kind: lax.all_gather(a.astype(kind), axis),
        shard,
        (jnp.bfloat16, jnp.bfloat16, jnp.bfloat16),
    )
    state = jax.tree.map(lambda a, e: jnp.zeros_like(a) + jnp.asarray(e, a.dtype), shard, neutral)

    def one(step, state):
        return join(
            state,
            jax.tree.map(
                lambda a, own: lax.dynamic_index_in_dim(a, step, 0, False).astype(own.dtype),
                gathered,
                shard,
            ),
        )

    return lax.fori_loop(0, place, one, state)


def doc_of(places, ends):
    return jnp.sum((places[:, None] >= ends[None, :]).astype(jnp.int32), axis=1)


def shards(streams, short_filter, decay_rate, residue, skip_gain, lengths, queries, keys):
    rows = streams.shape[1]
    width = streams.shape[2]
    modes = decay_rate.shape[1]
    index = lax.axis_index("ctx")
    first = index * rows
    ends = jnp.cumsum(lengths)
    places = first + jnp.arange(rows, dtype=jnp.int32)
    doc_here = doc_of(places, ends)
    doc_before = doc_of(jnp.reshape(first - 1, (1,)), ends)[0]
    reach_back = SHORT - 1
    rim = shifted(streams[:, rows - reach_back :, :], "ctx", 1)
    extended = jnp.concatenate([rim, streams], axis=1)
    doc_ext = doc_of(first - reach_back + jnp.arange(rows + reach_back, dtype=jnp.int32), ends)
    filtered = jnp.zeros(streams.shape, jnp.float32)
    for tap in range(SHORT):
        window = extended[:, reach_back - tap : reach_back - tap + rows, :].astype(jnp.float32)
        same = (doc_ext[reach_back - tap : reach_back - tap + rows] == doc_here).astype(jnp.float32)
        filtered = filtered + short_filter[tap][:, None, :] * window * same[None, :, None]
    mixed = filtered[1] * filtered[2]
    sub_len = math.gcd(rows, 16)
    blocks = rows // sub_len
    lags = jnp.arange(sub_len + 1, dtype=jnp.float32)
    powers = jnp.exp(-decay_rate[None] * lags[:, None, None])
    kernel = jnp.sum(residue[None] * powers[:sub_len], axis=2)
    padded = jnp.concatenate([kernel[::-1], jnp.zeros_like(kernel)], axis=0)
    tiled = jnp.tile(padded, (sub_len, 1))[: sub_len * (2 * sub_len - 1)]
    toeplitz = tiled.reshape(sub_len, 2 * sub_len - 1, width)[:, sub_len - 1 :, :]
    mixed_blocks = mixed.reshape(blocks, sub_len, width)
    doc_blocks = doc_here.reshape(blocks, sub_len)
    same_blocks = (doc_blocks[:, :, None] == doc_blocks[:, None, :]).astype(jnp.float32)
    local = jnp.sum(toeplitz[None] * same_blocks[..., None] * mixed_blocks[:, None, :, :], axis=2)
    prior = jnp.concatenate([doc_before.reshape(1), doc_blocks[:-1, -1]])
    in_last = (doc_blocks == doc_blocks[:, -1:]).astype(jnp.float32)
    ahead = powers[sub_len:0:-1]
    summaries = jnp.einsum(
        "bjc,jcm->bcm", mixed_blocks * in_last[..., None], ahead, precision=lax.Precision.HIGHEST
    )
    keeps = (doc_blocks[:, -1] == prior).astype(jnp.float32)
    step_decay = powers[sub_len]

    def advance(carry, item):
        state, factor = carry
        summary, keep = item
        gain = step_decay * keep
        return ((state * gain + summary, factor * gain), (state, factor))

    empty_state = jnp.zeros((width, modes), jnp.float32)
    (own_state, own_factor), (pre_state, pre_factor) = lax.scan(
        advance, (empty_state, jnp.ones((width, modes), jnp.float32)), (summaries, keeps)
    )
    keep_device = jnp.prod(keeps)

    def combine(earlier, later):
        state_a, keep_a, count_a = earlier
        state_b, keep_b, count_b = later
        span = jnp.exp(-decay_rate * (rows * count_b))
        return (state_a * span * keep_b + state_b, keep_a * keep_b, count_a + count_b)

    incoming, keep_sum, count_sum = prefix(
        (own_state, keep_device, jnp.ones((), jnp.float32)),
        "ctx",
        combine,
        (empty_state, jnp.ones((), jnp.float32), jnp.zeros((), jnp.float32)),
    )
    starts = pre_state + pre_factor * incoming[None]
    carry_mask = (doc_blocks == prior[:, None]).astype(jnp.float32)
    cross = (
        jnp.einsum(
            "jcm,bcm->bjc",
            powers[:sub_len],
            residue[None] * starts,
            precision=lax.Precision.HIGHEST,
        )
        * carry_mask[..., None]
    )
    long = (local + cross).reshape(rows, width) + skip_gain[None, :] * mixed
    hyena_out = (filtered[0] * long).astype(jnp.bfloat16)
    heads_here = width // HEAD_DIM
    scale = 1.0 / math.sqrt(HEAD_DIM)
    query_docs = doc_of(places, ends)
    query_heads = queries.reshape(rows, heads_here, HEAD_DIM)
    paired = jnp.stack([keys, hyena_out])
    start_carry = (
        jnp.full((heads_here, rows), -1e30, jnp.float32),
        jnp.zeros((heads_here, rows), jnp.float32),
        jnp.zeros((heads_here, rows, HEAD_DIM), jnp.float32),
    )
    piece = lax.all_gather(paired, "ctx", axis=1, tiled=True)
    count = piece.shape[1]
    key_places = jnp.arange(count, dtype=jnp.int32)
    key_docs = doc_of(key_places, ends)
    allowed = (key_places[None, :] <= places[:, None]) & (key_docs[None, :] == query_docs[:, None])

    def compute(state):
        top, total, summed = state
        key_heads = piece[0].reshape(count, heads_here, HEAD_DIM)
        value_heads = piece[1].reshape(count, heads_here, HEAD_DIM)
        scores = jnp.einsum(
            "qhd,khd->hqk", query_heads, key_heads, preferred_element_type=jnp.float32
        )
        masked = jnp.where(allowed[None], scores * scale, -1e30)
        new_top = jnp.maximum(top, jnp.max(masked, axis=2))
        weight = jnp.exp(masked - new_top[..., None])
        total = jnp.sum(weight, axis=2)
        summed = jnp.einsum(
            "hqk,khd->hqd",
            weight.astype(jnp.bfloat16),
            value_heads,
            preferred_element_type=jnp.float32,
        )
        return (new_top, total, summed)

    def unchanged(state):
        return state

    result = lax.cond(jnp.any(allowed), compute, unchanged, start_carry)
    top, total, summed = result
    attended_rows = (
        (summed / total[..., None]).transpose(1, 0, 2).reshape(rows, width).astype(jnp.bfloat16)
    )
    return (hyena_out, attended_rows)


LANES = 128
SEGS = 8
PARTS = 4
NEG = -1e30
DIMS = (((1,), (1,)), ((), ()))


def fused_kernel(
    lengths, streams_far, taps_far, rate_far, residue_far, skip_far, queries_far, keys_far,
    hyena, attended, streams, taps, rate, residue, skip, queries, keys, ext, rim_out, rim_in, same, mixed_seg, gate_seg, starts, own, own_low, state_in, incoming,
    tokens, query_in, key_in, value_in, part_out, part_in, lse_out, lse_in, own_part, lse_rows, bias,
    rim_s, rim_r, state_s, state_r, query_s, query_r, key_s, key_r, value_s, value_r,
    part_s, part_r, lse_s, lse_r, load_s,
):
    me = lax.axis_index("ctx")
    rows, width = queries.shape
    heads = width // LANES
    modes = rate.shape[0]
    seg = rows // SEGS
    group = width // PARTS
    per = heads // PARTS
    first = me * rows

    def send(src, dst, s, r, to):
        return pltpu.make_async_remote_copy(
            src_ref=src, dst_ref=dst, send_sem=s, recv_sem=r,
            device_id={"ctx": to}, device_id_type=pl.DeviceIdType.MESH,
        )

    def cols(g):
        return pl.ds(g * group, group)

    def rim_copy(to):
        return send(rim_out, rim_in, rim_s, rim_r, to)

    def state_copy(source, g, to):
        return send(
            own_low.at[:, cols(g)], state_in.at[source, :, cols(g)],
            state_s.at[to, g], state_r.at[source, g], to,
        )

    def query_copy(slot, g, to):
        return send(
            queries_far.at[:, cols(g)], query_in.at[slot, :, cols(g)],
            query_s.at[to, g], query_r.at[slot, g], to,
        )

    def key_copy(g):
        return send(keys_far.at[:, cols(g)], key_in.at[:, cols(g)], key_s.at[g], key_r.at[g], 1)

    def value_copy(g):
        return send(hyena.at[:, cols(g)], value_in.at[:, cols(g)], value_s.at[g], value_r.at[g], 1)

    def part_copy(slot, source, g, to):
        return send(
            part_out.at[slot, :, cols(g)], part_in.at[source - 1, :, cols(g)],
            part_s.at[slot, g], part_r.at[source - 1, g], to,
        )

    def lse_copy(slot, source, g, to):
        return send(
            lse_out.at[slot, g], lse_in.at[source - 1, g], lse_s.at[slot, g], lse_r.at[source - 1, g], to
        )

    pairs = (
        (streams_far, streams), (rate_far, rate), (taps_far, taps), (residue_far, residue),
        (skip_far, skip), (keys_far, keys), (queries_far, queries),
    )
    loads = [pltpu.make_async_copy(far, near, load_s.at[n]) for n, (far, near) in enumerate(pairs)]
    for load in loads:
        load.start()

    barrier = pltpu.get_barrier_semaphore()
    for away in range(1, 4):
        pl.semaphore_signal(
            barrier, inc=1, device_id={"ctx": lax.rem(me + away, 4)},
            device_id_type=pl.DeviceIdType.MESH,
        )
    loads[0].wait()
    for j in range(3):
        rim_out[2 * j : 2 * j + 2, :] = streams[j, rows - 16 :, :].astype(jnp.float32)[14:16]
    rim_out[6:8, :] = jnp.zeros((2, width), jnp.float32)
    pl.semaphore_wait(barrier, 3)

    for i in range(3):
        @pl.when(me == i)
        def _():
            rim_copy(i + 1).start()

    @pl.when(me == 0)
    def _():
        for g in range(PARTS):
            key_copy(g).start()

    @pl.when(me == 2)
    def _():
        for g in range(PARTS):
            query_copy(0, g, 1).start()

    @pl.when(me == 3)
    def _():
        for g in range(PARTS):
            query_copy(1, g, 1).start()
            query_copy(1, g, 2).start()

    ends = []
    total = jnp.int32(0)
    for r in range(lengths.shape[0]):
        total = total + lengths[r]
        ends.append(total)

    def doc(places):
        found = jnp.zeros(places.shape, jnp.int32)
        for end in ends:
            found = found + (places >= end).astype(jnp.int32)
        return found

    def equal(a, b):
        return (doc(a) == doc(b)).astype(jnp.float32)

    segment = lax.broadcasted_iota(jnp.int32, (SEGS, LANES), 0)
    for t in range(seg):
        at = first + segment * seg + t
        same[0, t] = equal(at, at - 1)
        same[1, t] = equal(at, at - 2)
    last = first + segment * seg + (seg - 1)
    windows = [
        equal(last, last - span * seg) * (segment >= span).astype(jnp.float32) for span in (1, 2, 4)
    ]
    before = segment * 0 + (first - 1)
    carried = equal(first + segment * seg - 1, before)

    @pl.when(me == 0)
    def _():
        rim_in[...] = jnp.zeros(rim_in.shape, jnp.float32)

    for i in range(1, 4):
        @pl.when(me == i)
        def _():
            rim_copy(i - 1).wait_recv()

    for load in loads[1:]:
        load.wait()

    def spread(value):
        return jnp.broadcast_to(value[:, None, :], (modes, SEGS, LANES))

    def forward(h, _):
        lanes = pl.ds(pl.multiple_of(h * LANES, LANES), LANES)
        for j in range(3):
            ext[j, h, 8:, :] = streams[j, :, lanes].astype(jnp.float32)
            ext[j, h, 6:8, :] = rim_in[2 * j : 2 * j + 2, lanes]
        speed = rate[:, lanes]
        decay = spread(jnp.exp(-speed))
        gains = [
            [jnp.broadcast_to(taps[i, j : j + 1, lanes], (SEGS, LANES)) for j in range(3)]
            for i in range(3)
        ]
        older = [ext[j, h, pl.ds(6, SEGS, stride=seg), :] for j in range(3)]
        newer = [ext[j, h, pl.ds(7, SEGS, stride=seg), :] for j in range(3)]
        state = jnp.zeros((modes, SEGS, LANES), jnp.float32)
        for t in range(seg):
            here = [ext[j, h, pl.ds(8 + t, SEGS, stride=seg), :] for j in range(3)]
            near, far = same[0, t], same[1, t]
            out = [
                gains[0][j] * here[j] + gains[1][j] * (newer[j] * near) + gains[2][j] * (older[j] * far)
                for j in range(3)
            ]
            mixed = out[1] * out[2]
            gate_seg[h, t] = out[0]
            mixed_seg[h, t] = mixed
            state = state * near[None] * decay + mixed[None]
            older, newer = newer, here
        for window, span in zip(windows, (1, 2, 4)):
            step = spread(jnp.exp(-speed * float(span * seg)))
            state = state + step * window[None] * pltpu.roll(state, span, 1)
        for m in range(modes):
            own[m : m + 1, lanes] = state[m, SEGS - 1 :, :]
        starts[h] = pltpu.roll(state, 1, 1) * (segment >= 1).astype(jnp.float32)[None]
        return _

    edge = jnp.zeros((1, LANES), jnp.int32)

    def forward_group(g):
        lax.fori_loop(g * per, (g + 1) * per, forward, 0)
        own_low[:, cols(g)] = own[:, cols(g)].astype(jnp.bfloat16)
        for i in range(3):
            @pl.when(me == i)
            def _():
                for to in range(i + 1, 4):
                    state_copy(i, g, to).start()

    def receive_group(g):
        incoming[:, cols(g)] = jnp.zeros((modes, group), jnp.float32)
        for i in range(1, 4):
            @pl.when(me == i)
            def _():
                for j in range(i - 1, -1, -1):
                    state_copy(j, g, i).wait_recv()
                    linked = equal(edge + (j + 1) * rows - 1, edge + i * rows - 1)
                    linked = jnp.concatenate([linked] * per, axis=1)
                    span = jnp.exp(-rate[:, cols(g)] * float(rows * (i - 1 - j))) * linked
                    arrived = state_in[j, :, cols(g)].astype(jnp.float32)
                    incoming[:, cols(g)] = incoming[:, cols(g)] + arrived * span

    age = (segment * seg).astype(jnp.float32)

    def backward(h, _):
        lanes = pl.ds(pl.multiple_of(h * LANES, LANES), LANES)
        speed = spread(rate[:, lanes])
        decay = spread(jnp.exp(-rate[:, lanes]))
        weight = spread(residue[:, lanes])
        direct = jnp.broadcast_to(skip[:, lanes], (SEGS, LANES))
        state = starts[h] + spread(incoming[:, lanes]) * (jnp.exp(-speed * age[None]) * carried[None])
        for t in range(seg):
            mixed = mixed_seg[h, t]
            state = state * same[0, t][None] * decay + mixed[None]
            long = jnp.sum(weight * state, axis=0) + direct * mixed
            tokens[pl.ds(t, SEGS, stride=seg), :] = gate_seg[h, t] * long
        hyena[:, lanes] = tokens[...].astype(jnp.bfloat16)
        return _

    scale = 1.0 / math.sqrt(HEAD_DIM)
    lane = lax.broadcasted_iota(jnp.int32, (rows, LANES), 1)
    down = lax.broadcasted_iota(jnp.int32, (rows, rows), 0)
    across = lax.broadcasted_iota(jnp.int32, (rows, rows), 1)
    lse_rows[...] = jnp.zeros(lse_rows.shape, jnp.float32)

    def set_bias(query_block, key_block, a, b):
        p = query_block * rows + down
        q = key_block * rows + across
        allowed = (q <= p) & (doc(p) == doc(q))
        bias[a * rows : (a + 1) * rows, b * rows : (b + 1) * rows] = jnp.where(allowed, 0.0, NEG)

    def attend(query, key, value, penalty):
        scores = lax.dot_general(query, key, DIMS, preferred_element_type=jnp.float32)
        scores = scores * scale + penalty
        top = jnp.max(scores, axis=1, keepdims=True)
        weight = jnp.exp(scores - top)
        total = jnp.sum(weight, axis=1, keepdims=True)
        summed = jnp.dot(weight.astype(jnp.bfloat16), value, preferred_element_type=jnp.float32)
        return summed * (1.0 / total), top + jnp.log(total)

    def note(slot, g, h, value):
        lse_rows[slot, g] = jnp.where(lane == h - g * per, value, lse_rows[slot, g])

    def send_part(slot, source, g, to, table):
        lse_out[slot, g] = lse_rows[table, g].T[:SEGS]
        lse_copy(slot, source, g, to).start()
        part_copy(slot, source, g, to).start()

    def head_lanes(h):
        return pl.ds(pl.multiple_of(h * LANES, LANES), LANES)

    def attend_own(h, _):
        at = head_lanes(h)
        out, lse = attend(queries[:, at], keys[:, at], hyena[:, at], bias[:rows, :rows])
        attended[:, at] = out.astype(jnp.bfloat16)
        return _

    def attend_second(g, h, _):
        at = head_lanes(h)
        query = jnp.concatenate([query_in[0, :, at], query_in[1, :, at], queries[:, at]], axis=0)
        key = jnp.concatenate([key_in[:, at], keys[:, at]], axis=0)
        value = jnp.concatenate([value_in[:, at], hyena[:, at]], axis=0)
        out, lse = attend(query, key, value, bias[...])
        part_out[0, :, at] = out[:rows].astype(jnp.bfloat16)
        part_out[1, :, at] = out[rows : 2 * rows].astype(jnp.bfloat16)
        attended[:, at] = out[2 * rows :].astype(jnp.bfloat16)
        note(0, g, h, lse[:rows])
        note(1, g, h, lse[rows : 2 * rows])
        return _

    def attend_third(g, h, _):
        at = head_lanes(h)
        query = jnp.concatenate([query_in[1, :, at], queries[:, at]], axis=0)
        out, lse = attend(query, keys[:, at], hyena[:, at], bias[: 2 * rows, :rows])
        part_out[0, :, at] = out[:rows].astype(jnp.bfloat16)
        own_part[:, at] = out[rows:]
        note(1, g, h, lse[:rows])
        note(0, g, h, lse[rows:])
        return _

    def attend_last(g, h, _):
        at = head_lanes(h)
        out, lse = attend(queries[:, at], keys[:, at], hyena[:, at], bias[:rows, :rows])
        own_part[:, at] = out
        note(0, g, h, lse)
        return _

    def combine(sources, g):
        tables = [lse_rows[0, g]]
        for source in sources:
            lse_copy(0, source, g, 0).wait_recv()
            filler = jnp.zeros((LANES - SEGS, rows), jnp.float32)
            tables.append(jnp.concatenate([lse_in[source - 1, g], filler], axis=0).T)
        peak = functools.reduce(jnp.maximum, tables)
        shares = [jnp.exp(table - peak) for table in tables]
        norm = 1.0 / functools.reduce(jnp.add, shares)
        shares = [share * norm for share in shares]
        for source in sources:
            part_copy(0, source, g, 0).wait_recv()
        for n in range(per):
            at = slice((g * per + n) * LANES, (g * per + n + 1) * LANES)
            whole = own_part[:, at] * shares[0][:, n : n + 1]
            for share, source in zip(shares[1:], sources):
                whole = whole + part_in[source - 1, :, at].astype(jnp.float32) * share[:, n : n + 1]
            attended[:, at] = whole.astype(jnp.bfloat16)

    @pl.when(me == 0)
    def _():
        set_bias(0, 0, 0, 0)

    @pl.when(me == 1)
    def _():
        for a, query_block in enumerate((2, 3, 1)):
            for b in range(2):
                set_bias(query_block, b, a, b)

    @pl.when(me == 2)
    def _():
        set_bias(3, 2, 0, 0)
        set_bias(2, 2, 1, 0)

    @pl.when(me == 3)
    def _():
        set_bias(3, 3, 0, 0)

    forward_group(0)
    for g in range(PARTS):
        if g + 1 < PARTS:
            forward_group(g + 1)
        receive_group(g)
        lo, hi = g * per, (g + 1) * per
        lax.fori_loop(lo, hi, backward, 0)

        @pl.when(me == 0)
        def _():
            value_copy(g).start()
            lax.fori_loop(lo, hi, attend_own, 0)

        @pl.when(me == 1)
        def _():
            query_copy(0, g, 1).wait_recv()
            query_copy(1, g, 1).wait_recv()
            key_copy(g).wait_recv()
            value_copy(g).wait_recv()
            lax.fori_loop(lo, hi, functools.partial(attend_second, g), 0)
            send_part(0, 1, g, 2, 0)
            send_part(1, 1, g, 3, 1)

        @pl.when(me == 2)
        def _():
            query_copy(1, g, 2).wait_recv()
            lax.fori_loop(lo, hi, functools.partial(attend_third, g), 0)
            send_part(0, 2, g, 3, 1)

        @pl.when(me == 3)
        def _():
            lax.fori_loop(lo, hi, functools.partial(attend_last, g), 0)

    for g in range(PARTS):
        @pl.when(me == 0)
        def _():
            key_copy(g).wait_send()
            value_copy(g).wait_send()

        @pl.when(me == 1)
        def _():
            for slot in range(2):
                part_copy(slot, 1, g, slot + 2).wait_send()
                lse_copy(slot, 1, g, slot + 2).wait_send()

        @pl.when(me == 2)
        def _():
            combine((1,), g)
            query_copy(0, g, 1).wait_send()
            part_copy(0, 2, g, 3).wait_send()
            lse_copy(0, 2, g, 3).wait_send()

        @pl.when(me == 3)
        def _():
            combine((2, 1), g)
            query_copy(1, g, 1).wait_send()
            query_copy(1, g, 2).wait_send()

    for i in range(3):
        @pl.when(me == i)
        def _():
            rim_copy(i + 1).wait_send()
            for to in range(i + 1, 4):
                for g in range(PARTS):
                    state_copy(i, g, to).wait_send()


def fused(streams, short_filter, decay_rate, residue, skip_gain, lengths, queries, keys):
    rows, width = queries.shape
    heads = width // LANES
    modes = decay_rate.shape[1]
    seg = rows // SEGS
    f32, bf16 = jnp.float32, jnp.bfloat16
    vmem, dma = pltpu.VMEM, pltpu.SemaphoreType.DMA
    block = pl.BlockSpec(memory_space=pltpu.VMEM)
    far = pl.BlockSpec(memory_space=pltpu.HBM)
    out = jax.ShapeDtypeStruct((rows, width), bf16)
    return pl.pallas_call(
        fused_kernel,
        out_shape=(out, out),
        in_specs=[pl.BlockSpec(memory_space=pltpu.SMEM)] + [far] * 7,
        out_specs=(block, block),
        scratch_shapes=[
            vmem(streams.shape, bf16),
            vmem(short_filter.shape, f32),
            vmem((modes, width), f32),
            vmem((modes, width), f32),
            vmem((1, width), f32),
            vmem((rows, width), bf16),
            vmem((rows, width), bf16),
            vmem((3, heads, rows + 8, LANES), f32),
            vmem((8, width), f32),
            vmem((8, width), f32),
            vmem((2, seg, SEGS, LANES), f32),
            vmem((heads, seg, SEGS, LANES), f32),
            vmem((heads, seg, SEGS, LANES), f32),
            vmem((heads, modes, SEGS, LANES), f32),
            vmem((modes, width), f32),
            vmem((modes, width), bf16),
            vmem((3, modes, width), bf16),
            vmem((modes, width), f32),
            vmem((rows, LANES), f32),
            vmem((2, rows, width), bf16),
            vmem((rows, width), bf16),
            vmem((rows, width), bf16),
            vmem((2, rows, width), bf16),
            vmem((2, rows, width), bf16),
            vmem((2, PARTS, SEGS, rows), f32),
            vmem((2, PARTS, SEGS, rows), f32),
            vmem((rows, width), f32),
            vmem((2, PARTS, rows, LANES), f32),
            vmem((3 * rows, 2 * rows), f32),
            dma, dma, dma((4, PARTS)), dma((3, PARTS)), dma((4, PARTS)), dma((2, PARTS)),
            dma((PARTS,)), dma((PARTS,)), dma((PARTS,)), dma((PARTS,)),
            dma((2, PARTS)), dma((2, PARTS)), dma((2, PARTS)), dma((2, PARTS)), dma((7,)),
        ],
        compiler_params=pltpu.CompilerParams(
            collective_id=0, has_side_effects=True, vmem_limit_bytes=60 * 1024 * 1024
        ),
        cost_estimate=pl.CostEstimate(
            flops=12 * rows * rows * width, bytes_accessed=14 * rows * width, transcendentals=0
        ),
    )(
        lengths, streams, short_filter, decay_rate.T, residue.T, skip_gain.reshape(1, width),
        queries, keys,
    )


def chosen(streams, *rest):
    if lax.axis_size("ctx") == 4 and streams.shape[1] == 128 and streams.shape[2] % 512 == 0:
        return fused(streams, *rest)
    return shards(streams, *rest)


def solution(mesh):
    placed = (
        P(None, ("groups", "ctx"), "tp"),
        P(None, None, "tp"),
        P("tp", None),
        P("tp", None),
        P("tp"),
        P("groups"),
        P(("groups", "ctx"), "tp"),
        P(("groups", "ctx"), "tp"),
    )
    return jax.shard_map(
        chosen,
        mesh=mesh,
        in_specs=placed,
        out_specs=(P(("groups", "ctx"), "tp"), P(("groups", "ctx"), "tp")),
        check_vma=False,
    )
```

```python
import functools
import math

import jax
import jax.numpy as jnp
from jax import lax
from jax.experimental import pallas as pl
from jax.experimental.pallas import tpu as pltpu
from jax.sharding import PartitionSpec as P

HEAD_DIM = 128
SHORT = 3


def shifted(value, axis, steps):
    count = lax.axis_size(axis)
    leading, last = (max(0, -steps), min(count, count - steps))
    return lax.ppermute(value, axis, [(source, source + steps) for source in range(leading, last)])


def prefix(shard, axis, join, neutral):
    place = lax.axis_index(axis)
    gathered = jax.tree.map(
        lambda a, kind: lax.all_gather(a.astype(kind), axis),
        shard,
        (jnp.bfloat16, jnp.bfloat16, jnp.bfloat16),
    )
    state = jax.tree.map(lambda a, e: jnp.zeros_like(a) + jnp.asarray(e, a.dtype), shard, neutral)

    def one(step, state):
        return join(
            state,
            jax.tree.map(
                lambda a, own: lax.dynamic_index_in_dim(a, step, 0, False).astype(own.dtype),
                gathered,
                shard,
            ),
        )

    return lax.fori_loop(0, place, one, state)


def doc_of(places, ends):
    return jnp.sum((places[:, None] >= ends[None, :]).astype(jnp.int32), axis=1)


def shards(streams, short_filter, decay_rate, residue, skip_gain, lengths, queries, keys):
    rows = streams.shape[1]
    width = streams.shape[2]
    modes = decay_rate.shape[1]
    index = lax.axis_index("ctx")
    first = index * rows
    ends = jnp.cumsum(lengths)
    places = first + jnp.arange(rows, dtype=jnp.int32)
    doc_here = doc_of(places, ends)
    doc_before = doc_of(jnp.reshape(first - 1, (1,)), ends)[0]
    reach_back = SHORT - 1
    rim = shifted(streams[:, rows - reach_back :, :], "ctx", 1)
    extended = jnp.concatenate([rim, streams], axis=1)
    doc_ext = doc_of(first - reach_back + jnp.arange(rows + reach_back, dtype=jnp.int32), ends)
    filtered = jnp.zeros(streams.shape, jnp.float32)
    for tap in range(SHORT):
        window = extended[:, reach_back - tap : reach_back - tap + rows, :].astype(jnp.float32)
        same = (doc_ext[reach_back - tap : reach_back - tap + rows] == doc_here).astype(jnp.float32)
        filtered = filtered + short_filter[tap][:, None, :] * window * same[None, :, None]
    mixed = filtered[1] * filtered[2]
    sub_len = math.gcd(rows, 16)
    blocks = rows // sub_len
    lags = jnp.arange(sub_len + 1, dtype=jnp.float32)
    powers = jnp.exp(-decay_rate[None] * lags[:, None, None])
    kernel = jnp.sum(residue[None] * powers[:sub_len], axis=2)
    padded = jnp.concatenate([kernel[::-1], jnp.zeros_like(kernel)], axis=0)
    tiled = jnp.tile(padded, (sub_len, 1))[: sub_len * (2 * sub_len - 1)]
    toeplitz = tiled.reshape(sub_len, 2 * sub_len - 1, width)[:, sub_len - 1 :, :]
    mixed_blocks = mixed.reshape(blocks, sub_len, width)
    doc_blocks = doc_here.reshape(blocks, sub_len)
    same_blocks = (doc_blocks[:, :, None] == doc_blocks[:, None, :]).astype(jnp.float32)
    local = jnp.sum(toeplitz[None] * same_blocks[..., None] * mixed_blocks[:, None, :, :], axis=2)
    prior = jnp.concatenate([doc_before.reshape(1), doc_blocks[:-1, -1]])
    in_last = (doc_blocks == doc_blocks[:, -1:]).astype(jnp.float32)
    ahead = powers[sub_len:0:-1]
    summaries = jnp.einsum(
        "bjc,jcm->bcm", mixed_blocks * in_last[..., None], ahead, precision=lax.Precision.HIGHEST
    )
    keeps = (doc_blocks[:, -1] == prior).astype(jnp.float32)
    step_decay = powers[sub_len]

    def advance(carry, item):
        state, factor = carry
        summary, keep = item
        gain = step_decay * keep
        return ((state * gain + summary, factor * gain), (state, factor))

    empty_state = jnp.zeros((width, modes), jnp.float32)
    (own_state, own_factor), (pre_state, pre_factor) = lax.scan(
        advance, (empty_state, jnp.ones((width, modes), jnp.float32)), (summaries, keeps)
    )
    keep_device = jnp.prod(keeps)

    def combine(earlier, later):
        state_a, keep_a, count_a = earlier
        state_b, keep_b, count_b = later
        span = jnp.exp(-decay_rate * (rows * count_b))
        return (state_a * span * keep_b + state_b, keep_a * keep_b, count_a + count_b)

    incoming, keep_sum, count_sum = prefix(
        (own_state, keep_device, jnp.ones((), jnp.float32)),
        "ctx",
        combine,
        (empty_state, jnp.ones((), jnp.float32), jnp.zeros((), jnp.float32)),
    )
    starts = pre_state + pre_factor * incoming[None]
    carry_mask = (doc_blocks == prior[:, None]).astype(jnp.float32)
    cross = (
        jnp.einsum(
            "jcm,bcm->bjc",
            powers[:sub_len],
            residue[None] * starts,
            precision=lax.Precision.HIGHEST,
        )
        * carry_mask[..., None]
    )
    long = (local + cross).reshape(rows, width) + skip_gain[None, :] * mixed
    hyena_out = (filtered[0] * long).astype(jnp.bfloat16)
    heads_here = width // HEAD_DIM
    scale = 1.0 / math.sqrt(HEAD_DIM)
    query_docs = doc_of(places, ends)
    query_heads = queries.reshape(rows, heads_here, HEAD_DIM)
    paired = jnp.stack([keys, hyena_out])
    start_carry = (
        jnp.full((heads_here, rows), -1e30, jnp.float32),
        jnp.zeros((heads_here, rows), jnp.float32),
        jnp.zeros((heads_here, rows, HEAD_DIM), jnp.float32),
    )
    piece = lax.all_gather(paired, "ctx", axis=1, tiled=True)
    count = piece.shape[1]
    key_places = jnp.arange(count, dtype=jnp.int32)
    key_docs = doc_of(key_places, ends)
    allowed = (key_places[None, :] <= places[:, None]) & (key_docs[None, :] == query_docs[:, None])

    def compute(state):
        top, total, summed = state
        key_heads = piece[0].reshape(count, heads_here, HEAD_DIM)
        value_heads = piece[1].reshape(count, heads_here, HEAD_DIM)
        scores = jnp.einsum(
            "qhd,khd->hqk", query_heads, key_heads, preferred_element_type=jnp.float32
        )
        masked = jnp.where(allowed[None], scores * scale, -1e30)
        new_top = jnp.maximum(top, jnp.max(masked, axis=2))
        weight = jnp.exp(masked - new_top[..., None])
        total = jnp.sum(weight, axis=2)
        summed = jnp.einsum(
            "hqk,khd->hqd",
            weight.astype(jnp.bfloat16),
            value_heads,
            preferred_element_type=jnp.float32,
        )
        return (new_top, total, summed)

    def unchanged(state):
        return state

    result = lax.cond(jnp.any(allowed), compute, unchanged, start_carry)
    top, total, summed = result
    attended_rows = (
        (summed / total[..., None]).transpose(1, 0, 2).reshape(rows, width).astype(jnp.bfloat16)
    )
    return (hyena_out, attended_rows)


LANES = 128
SEGS = 8
PARTS = 4
NEG = -1e30
DIMS = (((1,), (1,)), ((), ()))


def fused_kernel(
    lengths, streams_far, taps_far, rate_far, residue_far, skip_far, queries_far, keys_far,
    hyena, attended, streams, taps, rate, residue, skip, queries, keys, ext, rim_out, rim_in, same, mixed_seg, gate_seg, starts, own, own_low, state_in, incoming,
    tokens, query_in, key_in, value_in, part_out, part_in, lse_out, lse_in, own_part, lse_rows, bias,
    rim_s, rim_r, state_s, state_r, query_s, query_r, key_s, key_r, value_s, value_r,
    part_s, part_r, lse_s, lse_r, load_s,
):
    me = lax.axis_index("ctx")
    rows, width = queries.shape
    heads = width // LANES
    modes = rate.shape[0]
    seg = rows // SEGS
    group = width // PARTS
    per = heads // PARTS
    first = me * rows

    def send(src, dst, s, r, to):
        return pltpu.make_async_remote_copy(
            src_ref=src, dst_ref=dst, send_sem=s, recv_sem=r,
            device_id={"ctx": to}, device_id_type=pl.DeviceIdType.MESH,
        )

    def cols(g):
        return pl.ds(g * group, group)

    def rim_copy(to):
        return send(rim_out, rim_in, rim_s, rim_r, to)

    def state_copy(source, g, to):
        return send(
            own_low.at[:, cols(g)], state_in.at[source, :, cols(g)],
            state_s.at[to, g], state_r.at[source, g], to,
        )

    def query_copy(slot, g, to):
        return send(
            queries_far.at[:, cols(g)], query_in.at[slot, :, cols(g)],
            query_s.at[to, g], query_r.at[slot, g], to,
        )

    def key_copy(g):
        return send(keys_far.at[:, cols(g)], key_in.at[:, cols(g)], key_s.at[g], key_r.at[g], 1)

    def value_copy(g):
        return send(hyena.at[:, cols(g)], value_in.at[:, cols(g)], value_s.at[g], value_r.at[g], 1)

    def part_copy(slot, source, g, to):
        return send(
            part_out.at[slot, :, cols(g)], part_in.at[source - 1, :, cols(g)],
            part_s.at[slot, g], part_r.at[source - 1, g], to,
        )

    def lse_copy(slot, source, g, to):
        return send(
            lse_out.at[slot, g], lse_in.at[source - 1, g], lse_s.at[slot, g], lse_r.at[source - 1, g], to
        )

    pairs = (
        (streams_far, streams), (rate_far, rate), (taps_far, taps), (residue_far, residue),
        (skip_far, skip), (keys_far, keys), (queries_far, queries),
    )
    loads = [pltpu.make_async_copy(far, near, load_s.at[n]) for n, (far, near) in enumerate(pairs)]
    for load in loads:
        load.start()

    barrier = pltpu.get_barrier_semaphore()
    for away in range(1, 4):
        pl.semaphore_signal(
            barrier, inc=1, device_id={"ctx": lax.rem(me + away, 4)},
            device_id_type=pl.DeviceIdType.MESH,
        )
    loads[0].wait()
    for j in range(3):
        rim_out[2 * j : 2 * j + 2, :] = streams[j, rows - 16 :, :].astype(jnp.float32)[14:16]
    rim_out[6:8, :] = jnp.zeros((2, width), jnp.float32)
    pl.semaphore_wait(barrier, 3)

    for i in range(3):
        @pl.when(me == i)
        def _():
            rim_copy(i + 1).start()

    @pl.when(me == 0)
    def _():
        for g in range(PARTS):
            key_copy(g).start()

    @pl.when(me == 2)
    def _():
        for g in range(PARTS):
            query_copy(0, g, 1).start()

    @pl.when(me == 3)
    def _():
        for g in range(PARTS):
            query_copy(1, g, 1).start()
            query_copy(1, g, 2).start()

    ends = []
    total = jnp.int32(0)
    for r in range(lengths.shape[0]):
        total = total + lengths[r]
        ends.append(total)

    def doc(places):
        found = jnp.zeros(places.shape, jnp.int32)
        for end in ends:
            found = found + (places >= end).astype(jnp.int32)
        return found

    def equal(a, b):
        return (doc(a) == doc(b)).astype(jnp.float32)

    segment = lax.broadcasted_iota(jnp.int32, (SEGS, LANES), 0)
    for t in range(seg):
        at = first + segment * seg + t
        same[0, t] = equal(at, at - 1)
        same[1, t] = equal(at, at - 2)
    last = first + segment * seg + (seg - 1)
    windows = [
        equal(last, last - span * seg) * (segment >= span).astype(jnp.float32) for span in (1, 2, 4)
    ]
    before = segment * 0 + (first - 1)
    carried = equal(first + segment * seg - 1, before)

    @pl.when(me == 0)
    def _():
        rim_in[...] = jnp.zeros(rim_in.shape, jnp.float32)

    for i in range(1, 4):
        @pl.when(me == i)
        def _():
            rim_copy(i - 1).wait_recv()

    for load in loads[1:]:
        load.wait()

    def spread(value):
        return jnp.broadcast_to(value[:, None, :], (modes, SEGS, LANES))

    def forward(h, _):
        lanes = pl.ds(pl.multiple_of(h * LANES, LANES), LANES)
        for j in range(3):
            ext[j, h, 8:, :] = streams[j, :, lanes].astype(jnp.float32)
            ext[j, h, 6:8, :] = rim_in[2 * j : 2 * j + 2, lanes]
        speed = rate[:, lanes]
        decay = spread(jnp.exp(-speed))
        gains = [
            [jnp.broadcast_to(taps[i, j : j + 1, lanes], (SEGS, LANES)) for j in range(3)]
            for i in range(3)
        ]
        older = [ext[j, h, pl.ds(6, SEGS, stride=seg), :] for j in range(3)]
        newer = [ext[j, h, pl.ds(7, SEGS, stride=seg), :] for j in range(3)]
        state = jnp.zeros((modes, SEGS, LANES), jnp.float32)
        for t in range(seg):
            here = [ext[j, h, pl.ds(8 + t, SEGS, stride=seg), :] for j in range(3)]
            near, far = same[0, t], same[1, t]
            out = [
                gains[0][j] * here[j] + gains[1][j] * (newer[j] * near) + gains[2][j] * (older[j] * far)
                for j in range(3)
            ]
            mixed = out[1] * out[2]
            gate_seg[h, t] = out[0]
            mixed_seg[h, t] = mixed
            state = state * near[None] * decay + mixed[None]
            older, newer = newer, here
        for window, span in zip(windows, (1, 2, 4)):
            step = spread(jnp.exp(-speed * float(span * seg)))
            state = state + step * window[None] * pltpu.roll(state, span, 1)
        for m in range(modes):
            own[m : m + 1, lanes] = state[m, SEGS - 1 :, :]
        starts[h] = pltpu.roll(state, 1, 1) * (segment >= 1).astype(jnp.float32)[None]
        return _

    edge = jnp.zeros((1, LANES), jnp.int32)

    def forward_group(g):
        lax.fori_loop(g * per, (g + 1) * per, forward, 0)
        own_low[:, cols(g)] = own[:, cols(g)].astype(jnp.bfloat16)
        for i in range(3):
            @pl.when(me == i)
            def _():
                for to in range(i + 1, 4):
                    state_copy(i, g, to).start()

    def receive_group(g):
        incoming[:, cols(g)] = jnp.zeros((modes, group), jnp.float32)
        for i in range(1, 4):
            @pl.when(me == i)
            def _():
                for j in range(i - 1, -1, -1):
                    state_copy(j, g, i).wait_recv()
                    linked = equal(edge + (j + 1) * rows - 1, edge + i * rows - 1)
                    linked = jnp.concatenate([linked] * per, axis=1)
                    span = jnp.exp(-rate[:, cols(g)] * float(rows * (i - 1 - j))) * linked
                    arrived = state_in[j, :, cols(g)].astype(jnp.float32)
                    incoming[:, cols(g)] = incoming[:, cols(g)] + arrived * span

    age = (segment * seg).astype(jnp.float32)

    def backward(h, _):
        lanes = pl.ds(pl.multiple_of(h * LANES, LANES), LANES)
        speed = spread(rate[:, lanes])
        decay = spread(jnp.exp(-rate[:, lanes]))
        weight = spread(residue[:, lanes])
        direct = jnp.broadcast_to(skip[:, lanes], (SEGS, LANES))
        state = starts[h] + spread(incoming[:, lanes]) * (jnp.exp(-speed * age[None]) * carried[None])
        for t in range(seg):
            mixed = mixed_seg[h, t]
            state = state * same[0, t][None] * decay + mixed[None]
            long = jnp.sum(weight * state, axis=0) + direct * mixed
            tokens[pl.ds(t, SEGS, stride=seg), :] = gate_seg[h, t] * long
        hyena[:, lanes] = tokens[...].astype(jnp.bfloat16)
        return _

    scale = 1.0 / math.sqrt(HEAD_DIM)
    lane = lax.broadcasted_iota(jnp.int32, (rows, LANES), 1)
    down = lax.broadcasted_iota(jnp.int32, (rows, rows), 0)
    across = lax.broadcasted_iota(jnp.int32, (rows, rows), 1)
    lse_rows[...] = jnp.zeros(lse_rows.shape, jnp.float32)

    def set_bias(query_block, key_block, a, b):
        p = query_block * rows + down
        q = key_block * rows + across
        allowed = (q <= p) & (doc(p) == doc(q))
        bias[a * rows : (a + 1) * rows, b * rows : (b + 1) * rows] = jnp.where(allowed, 0.0, NEG)

    def attend(query, key, value, penalty):
        scores = lax.dot_general(query, key, DIMS, preferred_element_type=jnp.float32)
        scores = scores * scale + penalty
        top = jnp.max(scores, axis=1, keepdims=True)
        weight = jnp.exp(scores - top)
        total = jnp.sum(weight, axis=1, keepdims=True)
        summed = jnp.dot(weight.astype(jnp.bfloat16), value, preferred_element_type=jnp.float32)
        return summed * (1.0 / total), top + jnp.log(total)

    def note(slot, g, h, value):
        lse_rows[slot, g] = jnp.where(lane == h - g * per, value, lse_rows[slot, g])

    def send_part(slot, source, g, to, table):
        lse_out[slot, g] = lse_rows[table, g].T[:SEGS]
        lse_copy(slot, source, g, to).start()
        part_copy(slot, source, g, to).start()

    def head_lanes(h):
        return pl.ds(h * LANES, LANES)

    def attend_own(h, _):
        at = head_lanes(h)
        out, lse = attend(queries[:, at], keys[:, at], hyena[:, at], bias[:rows, :rows])
        attended[:, at] = out.astype(jnp.bfloat16)
        return _

    def attend_second(g, h, _):
        at = head_lanes(h)
        query = jnp.concatenate([query_in[0, :, at], query_in[1, :, at], queries[:, at]], axis=0)
        key = jnp.concatenate([key_in[:, at], keys[:, at]], axis=0)
        value = jnp.concatenate([value_in[:, at], hyena[:, at]], axis=0)
        out, lse = attend(query, key, value, bias[...])
        part_out[0, :, at] = out[:rows].astype(jnp.bfloat16)
        part_out[1, :, at] = out[rows : 2 * rows].astype(jnp.bfloat16)
        attended[:, at] = out[2 * rows :].astype(jnp.bfloat16)
        note(0, g, h, lse[:rows])
        note(1, g, h, lse[rows : 2 * rows])
        return _

    def attend_third(g, h, _):
        at = head_lanes(h)
        query = jnp.concatenate([query_in[1, :, at], queries[:, at]], axis=0)
        out, lse = attend(query, keys[:, at], hyena[:, at], bias[: 2 * rows, :rows])
        part_out[0, :, at] = out[:rows].astype(jnp.bfloat16)
        own_part[:, at] = out[rows:]
        note(1, g, h, lse[:rows])
        note(0, g, h, lse[rows:])
        return _

    def attend_last(g, h, _):
        at = head_lanes(h)
        out, lse = attend(queries[:, at], keys[:, at], hyena[:, at], bias[:rows, :rows])
        own_part[:, at] = out
        note(0, g, h, lse)
        return _

    def combine(sources, g):
        tables = [lse_rows[0, g]]
        for source in sources:
            lse_copy(0, source, g, 0).wait_recv()
            filler = jnp.zeros((LANES - SEGS, rows), jnp.float32)
            tables.append(jnp.concatenate([lse_in[source - 1, g], filler], axis=0).T)
        peak = functools.reduce(jnp.maximum, tables)
        shares = [jnp.exp(table - peak) for table in tables]
        norm = 1.0 / functools.reduce(jnp.add, shares)
        shares = [share * norm for share in shares]
        for source in sources:
            part_copy(0, source, g, 0).wait_recv()
        for n in range(per):
            at = slice((g * per + n) * LANES, (g * per + n + 1) * LANES)
            whole = own_part[:, at] * shares[0][:, n : n + 1]
            for share, source in zip(shares[1:], sources):
                whole = whole + part_in[source - 1, :, at].astype(jnp.float32) * share[:, n : n + 1]
            attended[:, at] = whole.astype(jnp.bfloat16)

    @pl.when(me == 0)
    def _():
        set_bias(0, 0, 0, 0)

    @pl.when(me == 1)
    def _():
        for a, query_block in enumerate((2, 3, 1)):
            for b in range(2):
                set_bias(query_block, b, a, b)

    @pl.when(me == 2)
    def _():
        set_bias(3, 2, 0, 0)
        set_bias(2, 2, 1, 0)

    @pl.when(me == 3)
    def _():
        set_bias(3, 3, 0, 0)

    forward_group(0)
    for g in range(PARTS):
        if g + 1 < PARTS:
            forward_group(g + 1)
        receive_group(g)
        lo, hi = g * per, (g + 1) * per
        lax.fori_loop(lo, hi, backward, 0)

        @pl.when(me == 0)
        def _():
            value_copy(g).start()
            for h in range(lo, hi):
                attend_own(h, 0)

        @pl.when(me == 1)
        def _():
            query_copy(0, g, 1).wait_recv()
            query_copy(1, g, 1).wait_recv()
            key_copy(g).wait_recv()
            value_copy(g).wait_recv()
            for h in range(lo, hi):
                attend_second(g, h, 0)
            send_part(0, 1, g, 2, 0)
            send_part(1, 1, g, 3, 1)

        @pl.when(me == 2)
        def _():
            query_copy(1, g, 2).wait_recv()
            for h in range(lo, hi):
                attend_third(g, h, 0)
            send_part(0, 2, g, 3, 1)

        @pl.when(me == 3)
        def _():
            for h in range(lo, hi):
                attend_last(g, h, 0)

    for g in range(PARTS):
        @pl.when(me == 0)
        def _():
            key_copy(g).wait_send()
            value_copy(g).wait_send()

        @pl.when(me == 1)
        def _():
            for slot in range(2):
                part_copy(slot, 1, g, slot + 2).wait_send()
                lse_copy(slot, 1, g, slot + 2).wait_send()

        @pl.when(me == 2)
        def _():
            combine((1,), g)
            query_copy(0, g, 1).wait_send()
            part_copy(0, 2, g, 3).wait_send()
            lse_copy(0, 2, g, 3).wait_send()

        @pl.when(me == 3)
        def _():
            combine((2, 1), g)
            query_copy(1, g, 1).wait_send()
            query_copy(1, g, 2).wait_send()

    for i in range(3):
        @pl.when(me == i)
        def _():
            rim_copy(i + 1).wait_send()
            for to in range(i + 1, 4):
                for g in range(PARTS):
                    state_copy(i, g, to).wait_send()


def fused(streams, short_filter, decay_rate, residue, skip_gain, lengths, queries, keys):
    rows, width = queries.shape
    heads = width // LANES
    modes = decay_rate.shape[1]
    seg = rows // SEGS
    f32, bf16 = jnp.float32, jnp.bfloat16
    vmem, dma = pltpu.VMEM, pltpu.SemaphoreType.DMA
    block = pl.BlockSpec(memory_space=pltpu.VMEM)
    far = pl.BlockSpec(memory_space=pltpu.HBM)
    out = jax.ShapeDtypeStruct((rows, width), bf16)
    return pl.pallas_call(
        fused_kernel,
        out_shape=(out, out),
        in_specs=[pl.BlockSpec(memory_space=pltpu.SMEM)] + [far] * 7,
        out_specs=(block, block),
        scratch_shapes=[
            vmem(streams.shape, bf16),
            vmem(short_filter.shape, f32),
            vmem((modes, width), f32),
            vmem((modes, width), f32),
            vmem((1, width), f32),
            vmem((rows, width), bf16),
            vmem((rows, width), bf16),
            vmem((3, heads, rows + 8, LANES), f32),
            vmem((8, width), f32),
            vmem((8, width), f32),
            vmem((2, seg, SEGS, LANES), f32),
            vmem((heads, seg, SEGS, LANES), f32),
            vmem((heads, seg, SEGS, LANES), f32),
            vmem((heads, modes, SEGS, LANES), f32),
            vmem((modes, width), f32),
            vmem((modes, width), bf16),
            vmem((3, modes, width), bf16),
            vmem((modes, width), f32),
            vmem((rows, LANES), f32),
            vmem((2, rows, width), bf16),
            vmem((rows, width), bf16),
            vmem((rows, width), bf16),
            vmem((2, rows, width), bf16),
            vmem((2, rows, width), bf16),
            vmem((2, PARTS, SEGS, rows), f32),
            vmem((2, PARTS, SEGS, rows), f32),
            vmem((rows, width), f32),
            vmem((2, PARTS, rows, LANES), f32),
            vmem((3 * rows, 2 * rows), f32),
            dma, dma, dma((4, PARTS)), dma((3, PARTS)), dma((4, PARTS)), dma((2, PARTS)),
            dma((PARTS,)), dma((PARTS,)), dma((PARTS,)), dma((PARTS,)),
            dma((2, PARTS)), dma((2, PARTS)), dma((2, PARTS)), dma((2, PARTS)), dma((7,)),
        ],
        compiler_params=pltpu.CompilerParams(
            collective_id=0, has_side_effects=True, vmem_limit_bytes=60 * 1024 * 1024
        ),
        cost_estimate=pl.CostEstimate(
            flops=12 * rows * rows * width, bytes_accessed=14 * rows * width, transcendentals=0
        ),
    )(
        lengths, streams, short_filter, decay_rate.T, residue.T, skip_gain.reshape(1, width),
        queries, keys,
    )


def chosen(streams, *rest):
    if lax.axis_size("ctx") == 4 and streams.shape[1] == 128 and streams.shape[2] % 512 == 0:
        return fused(streams, *rest)
    return shards(streams, *rest)


def solution(mesh):
    placed = (
        P(None, ("groups", "ctx"), "tp"),
        P(None, None, "tp"),
        P("tp", None),
        P("tp", None),
        P("tp"),
        P("groups"),
        P(("groups", "ctx"), "tp"),
        P(("groups", "ctx"), "tp"),
    )
    return jax.shard_map(
        chosen,
        mesh=mesh,
        in_specs=placed,
        out_specs=(P(("groups", "ctx"), "tp"), P(("groups", "ctx"), "tp")),
        check_vma=False,
    )
```
